32 devices in a mesh: items: 16 (over z, y, core), seq: 2 (over x).
Axes of the slice: x: 2, y: 2, z: 4, core: 2. Of those that a mesh axis runs over, the one named last changes fastest.
Arguments:
- target_in: bfloat16 [64, 512, 1024], P('items', 'seq'), may hold values from -6 to 6
- memory: bfloat16 [64, 1024, 1024], P('items', 'seq'), may hold values from -6 to 6
- cotangent: bfloat16 [64, 512, 1024], P('items', 'seq'), may hold values from -6 to 6
- target_len: int32 [16, 4], P('items'), may hold values from 1 to 512, 1536 in all within a row
- memory_len: int32 [16, 4], P('items'), may hold values from 1 to 1024, 3072 in all within a row
- attn_in: bfloat16 [6, 1024, 1024], replicated, may hold values from -0.1875 to 0.1875
- attn_out: bfloat16 [2, 1024, 1024], replicated, may hold values from -0.75 to 0.75
- biases: float32 [7, 1024], replicated, may hold values from -3 to 3
- norm_gain: float32 [3, 1024], replicated, may hold values from 0.25 to 1.75
- norm_bias: float32 [3, 1024], replicated, may hold values from -3 to 3
- up_weight: bfloat16 [1024, 4096], P(None, 'seq'), may hold values from -0.1875 to 0.1875
- up_bias: float32 [4096], P('seq'), may hold values from -3 to 3
- down_weight: bfloat16 [1024, 4096], P(None, 'seq'), may hold values from -0.09375 to 0.09375
Outputs:
- layer_out: bfloat16 [64, 512, 1024], P('items', 'seq')
- target_grad: float32 [64, 512, 1024], P('items', 'seq')
- memory_grad: float32 [64, 1024, 1024], P('items', 'seq')
- attn_in_grad: float32 [6144, 1024], P(('items', 'seq'))
- attn_out_grad: float32 [2048, 1024], P(('items', 'seq'))
- bias_grad: float32 [7, 1024], replicated
- gain_grad: float32 [3, 1024], replicated
- norm_bias_grad: float32 [3, 1024], replicated
- up_grad: float32 [1024, 4096], P('items', 'seq')
- up_bias_grad: float32 [4096], replicated
- down_grad: float32 [1024, 4096], P('items', 'seq')
The draws below stay inside these ranges and needn't reach their ends.
Inputs may be any that keep to these rules, and one draw needn't show every extreme that they name: `target_len`: in each row of 4 lengths the sum is 1536 and the longest is 512. `memory_len`: in each row of 4 lengths the sum is 3072 and the longest is 1024.
All inputs are finite; a program needn't handle non-finite values.
Results may differ from the reference program's by a relative error of at most 0.02.
Values may be sent and summed in bfloat16 or wider, within the bound.
No kernel may reach another device: no remote copies, remote signals or barrier semaphores. Data moves between devices by JAX's collectives and lax.ppermute only.
A program may use at most 512 MiB of HBM per device.

```python
import math
import jax
import jax.numpy as jnp
import numpy as np
from jax import lax

D = 1024
H = 16
FF = 4096
TGT = 512
MEM = 1024
TAB = 4
GROUPS = 16
TABLES = 64


def block_scale(key, extent, split, least, largest):
    gain = 1.0
    for axis_at, blocks in split:
        draws = jax.random.uniform(jax.random.fold_in(jax.random.fold_in(key, 6), axis_at), (blocks,), jnp.float32, least / len(split), largest / len(split))
        gain = gain * jnp.repeat(jnp.exp(draws), extent[axis_at] // blocks).reshape((-1,) + (1,) * (len(extent) - 1 - axis_at))
    return gain


def profile(amount, total, most, skew):
    weights = [(1 << 20) // math.isqrt(grade ** skew) + 1 for grade in range(2, amount + 1)]
    spare, given = total - most - (amount - 1), [1] * (amount - 1)
    while spare > 0:
        movable = [i for i in range(amount - 1) if given[i] < most]
        mass, remaining = sum([weights[i] for i in movable]), spare
        for i in movable:
            more = min(most - given[i], max(1, remaining * weights[i] // mass), spare)
            given[i] = given[i] + more
            spare = spare - more
    return np.array([most] + given)


def uneven(stream_key, number_of, total, bound, lean):
    if number_of == 2:
        one = jax.random.randint(stream_key, (), max(1, total - bound), min(bound, total - 1) + 1)
        return jnp.stack([one, total - one])
    sizes = jnp.asarray(profile(number_of, total, bound, lean), jnp.int32)
    pairs = (number_of - 1) // 2
    source_of, taker = sizes[1:1 + 2 * pairs:2], sizes[2:2 + 2 * pairs:2]
    slack = jnp.minimum(source_of - 1, bound - taker)
    shifted = jax.random.randint(jax.random.fold_in(stream_key, 1), (pairs,), 0, 1 << 20) % (slack + 1)
    sizes = sizes.at[1:1 + 2 * pairs:2].set(source_of - shifted).at[2:2 + 2 * pairs:2].set(taker + shifted)
    return sizes[jax.random.permutation(jax.random.fold_in(stream_key, 2), number_of)]


def normal_values(own_key, shape, deviation, reach, cuts=(), dtype=jnp.bfloat16):
    array = jax.random.normal(own_key, shape, jnp.float32) * deviation
    if len(cuts) > 0:
        array = block_scale(own_key, shape, cuts, -0.22, 0.18) * array
    return jnp.clip(array, min=-reach, max=reach).astype(dtype)


def setup_inputs(seed: int = 0) -> dict:
    key_of = jax.random.split(jax.random.key(seed), 14)
    return {
        "target_in": normal_values(key_of[0], (TABLES, TGT, D), 1.0, 6.0, ((0, 16), (1, 2))),
        "memory": normal_values(key_of[1], (TABLES, MEM, D), 1.0, 6.0, ((0, 16), (1, 2))),
        "cotangent": normal_values(key_of[2], (TABLES, TGT, D), 1.0, 6.0, ((0, 16), (1, 2))),
        "target_len": jax.vmap(lambda own: uneven(own, TAB, TAB * TGT * 3 // 4, TGT, 2))(jax.random.split(key_of[3], GROUPS)).reshape((GROUPS, TAB)).astype(jnp.int32),
        "memory_len": jax.vmap(lambda own: uneven(own, TAB, TAB * MEM * 3 // 4, MEM, 2))(jax.random.split(key_of[4], GROUPS)).reshape((GROUPS, TAB)).astype(jnp.int32),
        "attn_in": normal_values(key_of[5], (6, D, D), D ** -0.5, 0.1875),
        "attn_out": normal_values(key_of[6], (2, D, D), (D // 16) ** -0.5, 0.75),
        "biases": normal_values(key_of[7], (7, D), 0.5, 3.0, (), jnp.float32),
        "norm_gain": jnp.clip(1.0 + 0.15 * jax.random.normal(key_of[8], (3, D), jnp.float32), 0.25, 1.75),
        "norm_bias": normal_values(key_of[9], (3, D), 0.5, 3.0, (), jnp.float32),
        "up_weight": normal_values(key_of[10], (D, FF), D ** -0.5, 0.1875, ((1, 2),)),
        "up_bias": normal_values(key_of[11], (FF,), 0.5, 3.0, ((0, 2),), jnp.float32),
        "down_weight": normal_values(key_of[12], (D, FF), FF ** -0.5, 0.09375, ((1, 2),)),
    }


@jax.custom_vjp
def low(v):
    return lax.optimization_barrier(v.astype(jnp.bfloat16)).astype(jnp.float32)

@jax.custom_vjp
def low_back(v):
    return v

def low_keep(v):
    return (low(v), None)

def low_pass(kept, grad):
    return (grad,)

def back_keep(v):
    return (v, None)

def back_low(kept, grad):
    return (low(grad),)
low.defvjp(low_keep, low_pass)
low_back.defvjp(back_keep, back_low)

def matmul(former, latter):
    return jnp.dot(former, latter, precision=lax.Precision.HIGHEST)

def both_low(argument):
    return low_back(low(argument))

def layer_norm(hidden, gain_row, shift_row):
    centre = hidden - lax.optimization_barrier(jnp.mean(hidden, axis=-1, keepdims=True))
    spread = lax.optimization_barrier(jnp.mean(centre * centre, axis=-1, keepdims=True))
    return centre * lax.rsqrt(spread + 1e-05) * gain_row + shift_row

def attend(queries, key_rows, value_rows, allowed):
    query_count = queries.shape[0]
    model_width = queries.shape[1]
    head_size = model_width // H
    score_scale = 1.0 / math.sqrt(head_size)
    scores = jnp.einsum('qhe,khe->hqk', queries.reshape(query_count, H, head_size), key_rows.reshape(-1, H, head_size), precision=lax.Precision.HIGHEST) * score_scale
    scores = jnp.where(allowed[None], scores, -1e+30)
    scores = low_back(scores)
    probability = jax.nn.softmax(scores, axis=-1)
    weights = low(probability)
    context = jnp.einsum('hqk,khe->qhe', weights, value_rows.reshape(-1, H, head_size), precision=lax.Precision.HIGHEST)
    return both_low(context.reshape(query_count, model_width))

def decoder_layer(params, target_rows, memory_rows, target_length, memory_length):
    attn_in, attn_out, biases, norm_gain, norm_bias, up_weight, up_bias, down_weight = params
    self_query = both_low(matmul(target_rows, attn_in[0]) + biases[0])
    self_keys = low(matmul(target_rows, attn_in[1]))
    self_values = low(matmul(target_rows, attn_in[2]) + biases[1])
    positions = jnp.arange(TGT)
    causal = (positions[None, :] <= positions[:, None]) & (positions[None, :] < target_length)
    self_context = attend(self_query, self_keys, self_values, causal)
    hidden_one = target_rows + low_back(matmul(self_context, attn_out[0]) + biases[2])
    norm_one = layer_norm(hidden_one, norm_gain[0], norm_bias[0])
    cross_query = both_low(matmul(low(norm_one), attn_in[3]) + biases[3])
    cross_keys = low(matmul(memory_rows, attn_in[4]))
    cross_values = low(matmul(memory_rows, attn_in[5]) + biases[4])
    visible = (jnp.arange(MEM) < memory_length)[None, :]
    cross_context = attend(cross_query, cross_keys, cross_values, visible)
    hidden_two = norm_one + low_back(matmul(cross_context, attn_out[1]) + biases[5])
    norm_two = layer_norm(hidden_two, norm_gain[1], norm_bias[1])
    up_act = low_back(matmul(low(norm_two), up_weight) + up_bias)
    up_out = low(jax.nn.gelu(up_act, approximate=False))
    ffn_out = low_back(matmul(up_out, down_weight.T) + biases[6])
    return layer_norm(norm_two + ffn_out, norm_gain[2], norm_bias[2])

def add_pair(former, latter):
    return former + latter

def reference(target_in, memory, cotangent, target_len, memory_len, attn_in, attn_out, biases, norm_gain, norm_bias, up_weight, up_bias, down_weight):
    params = tuple((array_in.astype(jnp.float32) for array_in in (attn_in, attn_out, biases, norm_gain, norm_bias, up_weight, up_bias, down_weight)))
    target_lengths = target_len.reshape(-1)
    memory_lengths = memory_len.reshape(-1)

    def one_table(totals, table_item):
        target_rows, memory_rows, outer_grad, target_length, memory_length = table_item

        def forward(weights, rows_in, mem_in):
            return decoder_layer(weights, rows_in, mem_in, target_length, memory_length)
        output, pull_back = jax.vjp(forward, params, target_rows.astype(jnp.float32), memory_rows.astype(jnp.float32))
        weight_grads, target_grad, memory_grad = pull_back(outer_grad.astype(jnp.float32))
        totals = jax.tree.map(add_pair, totals, weight_grads)
        return (totals, (output.astype(jnp.bfloat16), target_grad, memory_grad))
    zero_grads = jax.tree.map(jnp.zeros_like, params)
    totals, outputs = lax.scan(one_table, zero_grads, (target_in, memory, cotangent, target_lengths, memory_lengths))
    layer_out, target_grad, memory_grad = outputs
    return (layer_out, target_grad, memory_grad, totals[0].reshape(6 * D, D), totals[1].reshape(2 * D, D), totals[2], totals[3], totals[4], totals[5], totals[6], totals[7])
```

```python
import functools
import math

import jax
import jax.numpy as jnp
from jax import lax
from jax.experimental import pallas as pl
from jax.experimental.pallas import tpu as pltpu
from jax.sharding import PartitionSpec as P

H = 16


def layer_norm(hidden, gain_row, shift_row):
    centre = hidden - jnp.mean(hidden, axis=-1, keepdims=True)
    spread = jnp.mean(centre * centre, axis=-1, keepdims=True)
    return centre * lax.rsqrt(spread + 1e-05) * gain_row + shift_row


def gelu_exact(argument):
    return jax.nn.gelu(argument, approximate=False)


def project(hidden_rows, weight):
    return jnp.einsum("tld,de->tle", hidden_rows, weight, preferred_element_type=jnp.float32)


def project_back(gradient, weight):
    return jnp.einsum("tle,de->tld", gradient, weight, preferred_element_type=jnp.float32)


def exact_back(gradient, weight):
    return jnp.einsum(
        "tle,de->tld", gradient, weight.astype(jnp.float32), precision=lax.Precision.HIGHEST
    )


def outer_sum(former, latter):
    return jnp.einsum("tld,tle->de", former, latter, preferred_element_type=jnp.float32)


def exact_outer(former, latter):
    return jnp.einsum(
        "tld,tle->de", former.astype(jnp.float32), latter, precision=lax.Precision.HIGHEST
    )


def column_total(gradient):
    return jnp.sum(gradient.astype(jnp.float32), axis=(0, 1))


def split_heads(hidden_rows):
    return hidden_rows.reshape(
        hidden_rows.shape[0], hidden_rows.shape[1], H, hidden_rows.shape[2] // H
    )


def attn_scores(queries, key_rows, allowed):
    score_scale = 1.0 / math.sqrt(queries.shape[2] // H)
    scores = (
        jnp.einsum(
            "tqhe,tkhe->thqk",
            split_heads(queries),
            split_heads(key_rows),
            preferred_element_type=jnp.float32,
        )
        * score_scale
    )
    return jnp.where(allowed[:, None], scores, -1e30)


def attn_forward(queries, key_rows, value_rows, allowed):
    scores = attn_scores(queries, key_rows, allowed)
    row_top = jnp.max(scores, axis=-1, keepdims=True)
    exponent = jnp.exp(scores - row_top)
    row_total = jnp.sum(exponent, axis=-1, keepdims=True)
    probability = exponent / row_total
    context = jnp.einsum(
        "thqk,tkhe->tqhe",
        probability.astype(jnp.bfloat16),
        split_heads(value_rows),
        preferred_element_type=jnp.float32,
    )
    return (context.reshape(queries.shape).astype(jnp.bfloat16), row_top + jnp.log(row_total))


def attn_backward(queries, key_rows, value_rows, allowed, log_total, grad_context):
    score_scale = 1.0 / math.sqrt(queries.shape[2] // H)
    scores = attn_scores(queries, key_rows, allowed)
    probability = jnp.exp(scores - log_total)
    grad_heads = split_heads(grad_context)
    grad_values = jnp.einsum(
        "thqk,tqhe->tkhe",
        probability.astype(jnp.bfloat16),
        grad_heads,
        preferred_element_type=jnp.float32,
    )
    grad_probs = jnp.einsum(
        "tqhe,tkhe->thqk", grad_heads, split_heads(value_rows), preferred_element_type=jnp.float32
    )
    grad_scores = probability * (
        grad_probs - jnp.sum(probability * grad_probs, axis=-1, keepdims=True)
    )
    grad_scores = grad_scores.astype(jnp.bfloat16)
    grad_query = (
        jnp.einsum(
            "thqk,tkhe->tqhe",
            grad_scores,
            split_heads(key_rows),
            preferred_element_type=jnp.float32,
        )
        * score_scale
    )
    grad_keys = (
        jnp.einsum(
            "thqk,tqhe->tkhe", grad_scores, split_heads(queries), preferred_element_type=jnp.float32
        )
        * score_scale
    )
    return (
        grad_query.reshape(queries.shape).astype(jnp.bfloat16),
        grad_keys.reshape(key_rows.shape),
        grad_values.reshape(value_rows.shape),
    )


def on_device(
    target_in,
    memory,
    cotangent,
    target_len,
    memory_len,
    attn_in,
    attn_out,
    biases,
    norm_gain,
    norm_bias,
    up_weight,
    up_bias,
    down_weight,
):
    seq_count = lax.axis_size("seq")
    seq_place = lax.axis_index("seq")
    local_rows = target_in.shape[1]
    model_width = target_in.shape[2]
    full_rows = local_rows * seq_count
    memory_full = memory.shape[1] * seq_count
    hidden_local = up_weight.shape[1]
    target_length = target_len[0]
    memory_length = memory_len[0]
    query_place = seq_place * local_rows + jnp.arange(local_rows, dtype=jnp.int32)
    key_place = jnp.arange(full_rows, dtype=jnp.int32)
    causal = (key_place[None, None, :] <= query_place[None, :, None]) & (
        key_place[None, None, :] < target_length[:, None, None]
    )
    visible = jnp.arange(memory_full, dtype=jnp.int32)[None, None, :] < memory_length[:, None, None]
    self_query = (project(target_in, attn_in[0]) + biases[0]).astype(jnp.bfloat16)
    self_keys = project(target_in, attn_in[1]).astype(jnp.bfloat16)
    self_values = (project(target_in, attn_in[2]) + biases[1]).astype(jnp.bfloat16)
    all_keys, all_values = (
        lax.all_gather(self_keys, "seq", axis=1, tiled=True),
        lax.all_gather(self_values, "seq", axis=1, tiled=True),
    )
    self_context, self_total = attn_forward(self_query, all_keys, all_values, causal)
    hidden_one = target_in.astype(jnp.float32) + (project(self_context, attn_out[0]) + biases[2])
    norm_one = layer_norm(hidden_one, norm_gain[0], norm_bias[0])
    norm_one_low = norm_one.astype(jnp.bfloat16)
    cross_query = (project(norm_one_low, attn_in[3]) + biases[3]).astype(jnp.bfloat16)
    local_keys = project(memory, attn_in[4]).astype(jnp.bfloat16)
    local_values = (project(memory, attn_in[5]) + biases[4]).astype(jnp.bfloat16)
    cross_keys, cross_values = (
        lax.all_gather(local_keys, "seq", axis=1, tiled=True),
        lax.all_gather(local_values, "seq", axis=1, tiled=True),
    )
    cross_context, cross_total = attn_forward(cross_query, cross_keys, cross_values, visible)
    hidden_two = norm_one + (project(cross_context, attn_out[1]) + biases[5])
    norm_two = layer_norm(hidden_two, norm_gain[1], norm_bias[1])
    ffn_rows = lax.all_gather(norm_two.astype(jnp.bfloat16), "seq", axis=1, tiled=True)
    up_act = project(ffn_rows, up_weight) + up_bias
    up_out = gelu_exact(up_act).astype(jnp.bfloat16)
    ffn_sum = lax.psum_scatter(
        project_back(up_out, down_weight), "seq", scatter_dimension=1, tiled=True
    )
    hidden_three = norm_two + (ffn_sum + biases[6])
    final_rows, pull_three = jax.vjp(layer_norm, hidden_three, norm_gain[2], norm_bias[2])
    layer_out = final_rows.astype(jnp.bfloat16)
    grad_three, gain_three, shift_three = pull_three(cotangent.astype(jnp.float32))
    grad_ffn_out = grad_three.astype(jnp.bfloat16)
    grad_ffn_rows = lax.all_gather(grad_ffn_out, "seq", axis=1, tiled=True)
    grad_up_out = project(grad_ffn_rows, down_weight)
    unused_act, pull_gelu = jax.vjp(gelu_exact, up_act)
    grad_up_act = pull_gelu(grad_up_out)[0].astype(jnp.bfloat16)
    down_local = outer_sum(grad_ffn_rows, up_out)
    up_local = outer_sum(ffn_rows, grad_up_act)
    up_bias_local = column_total(grad_up_act)
    grad_norm_two = grad_three + lax.psum_scatter(
        project_back(grad_up_act, up_weight), "seq", scatter_dimension=1, tiled=True
    )
    unused_two, pull_two = jax.vjp(layer_norm, hidden_two, norm_gain[1], norm_bias[1])
    grad_two, gain_two, shift_two = pull_two(grad_norm_two)
    grad_cross_out = grad_two.astype(jnp.bfloat16)
    grad_cross_context = project_back(grad_cross_out, attn_out[1]).astype(jnp.bfloat16)
    grad_cross_query, cross_key_part, cross_value_part = attn_backward(
        cross_query, cross_keys, cross_values, visible, cross_total, grad_cross_context
    )
    key_grad, value_grad = (
        lax.psum_scatter(
            cross_key_part.astype(jnp.bfloat16), "seq", scatter_dimension=1, tiled=True
        ).astype(jnp.float32),
        lax.psum_scatter(
            cross_value_part.astype(jnp.bfloat16), "seq", scatter_dimension=1, tiled=True
        ).astype(jnp.float32),
    )
    memory_grad = exact_back(key_grad, attn_in[4]) + exact_back(value_grad, attn_in[5])
    memory_key_outer = exact_outer(memory, key_grad)
    memory_value_outer = exact_outer(memory, value_grad)
    cross_value_total = column_total(value_grad)
    grad_norm_one = grad_two + project_back(grad_cross_query, attn_in[3])
    unused_one, pull_one = jax.vjp(layer_norm, hidden_one, norm_gain[0], norm_bias[0])
    grad_one, gain_one, shift_one = pull_one(grad_norm_one)
    grad_self_out = grad_one.astype(jnp.bfloat16)
    grad_self_context = project_back(grad_self_out, attn_out[0]).astype(jnp.bfloat16)
    grad_self_query, self_key_part, self_value_part = attn_backward(
        self_query, all_keys, all_values, causal, self_total, grad_self_context
    )
    self_key_grad, self_value_grad = (
        lax.psum_scatter(
            self_key_part.astype(jnp.bfloat16), "seq", scatter_dimension=1, tiled=True
        ).astype(jnp.float32),
        lax.psum_scatter(
            self_value_part.astype(jnp.bfloat16), "seq", scatter_dimension=1, tiled=True
        ).astype(jnp.float32),
    )
    target_kv = exact_back(self_key_grad, attn_in[1]) + exact_back(self_value_grad, attn_in[2])
    self_key_outer = exact_outer(target_in, self_key_grad)
    self_value_outer = exact_outer(target_in, self_value_grad)
    self_value_total = column_total(self_value_grad)
    target_grad = grad_one + project_back(grad_self_query, attn_in[0]) + target_kv
    inner_grads = jnp.stack(
        [
            outer_sum(target_in, grad_self_query),
            self_key_outer,
            self_value_outer,
            outer_sum(norm_one_low, grad_cross_query),
            memory_key_outer,
            memory_value_outer,
        ]
    )
    outer_grads = jnp.stack(
        [outer_sum(self_context, grad_self_out), outer_sum(cross_context, grad_cross_out)]
    )
    attn_in_grad, attn_out_grad = (
        lax.psum_scatter(
            inner_grads.reshape(6 * model_width, model_width),
            ("items", "seq"),
            scatter_dimension=0,
            tiled=True,
        ),
        lax.psum_scatter(
            outer_grads.reshape(2 * model_width, model_width),
            ("items", "seq"),
            scatter_dimension=0,
            tiled=True,
        ),
    )
    up_grad, down_grad = (
        lax.psum_scatter(
            up_local.astype(jnp.bfloat16), "items", scatter_dimension=0, tiled=True
        ).astype(jnp.float32),
        lax.psum_scatter(
            down_local.astype(jnp.bfloat16), "items", scatter_dimension=0, tiled=True
        ).astype(jnp.float32),
    )
    bias_local = jnp.stack(
        [
            column_total(grad_self_query),
            self_value_total,
            column_total(grad_self_out),
            column_total(grad_cross_query),
            cross_value_total,
            column_total(grad_cross_out),
            column_total(grad_ffn_out),
        ]
    )
    gain_local = jnp.stack([gain_one, gain_two, gain_three])
    shift_local = jnp.stack([shift_one, shift_two, shift_three])
    up_bias_full = lax.dynamic_update_slice(
        jnp.zeros((hidden_local * seq_count,), jnp.float32),
        up_bias_local,
        (seq_place * hidden_local,),
    )
    bias_grad, gain_grad, norm_bias_grad, up_bias_grad = lax.psum(
        (bias_local, gain_local, shift_local, up_bias_full), ("items", "seq")
    )
    return (
        layer_out,
        target_grad,
        memory_grad,
        attn_in_grad,
        attn_out_grad,
        bias_grad,
        gain_grad,
        norm_bias_grad,
        up_grad,
        up_bias_grad,
        down_grad,
    )


NT = (((1,), (1,)), ((), ()))
NN = (((1,), (0,)), ((), ()))
TN = (((0,), (0,)), ((), ()))
LOG2E = 1.4426950408889634
LN2 = 0.6931471805599453
MASKED = -1e30


def dot32(former, latter, dims=NN):
    return lax.dot_general(former, latter, dims, preferred_element_type=jnp.float32)


def low(value):
    return value.astype(jnp.bfloat16)


def head_of_pair(rows, head):
    return lax.broadcasted_iota(jnp.int32, (rows, 128), 1) // 64 == head


def attend_kernel(length, q_ref, k_ref, v_ref, out_ref, total_ref, *, step, causal):
    valid = length[pl.program_id(0)]
    for at in range(0, q_ref.shape[1], step):
        seen = at + step if causal else k_ref.shape[1]
        queries, keys, values = q_ref[0, at : at + step, :], k_ref[0, :seen, :], v_ref[0, :seen, :]
        column = lax.broadcasted_iota(jnp.int32, (1, seen), 1)
        bias = jnp.where(column < valid, 0.0, MASKED).astype(jnp.float32)
        if causal:
            row = lax.broadcasted_iota(jnp.int32, (step, seen), 0) + at
            order = lax.broadcasted_iota(jnp.int32, (step, seen), 1) <= row
        for head in range(2):
            mine = head_of_pair(step, head)
            scores = dot32(jnp.where(mine, queries, jnp.zeros_like(queries)), keys, NT) + bias
            if causal:
                scores = jnp.where(order, scores, MASKED)
            top = jnp.max(scores, axis=1, keepdims=True)
            weight = jnp.exp2(scores - top)
            total = jnp.sum(weight, axis=1, keepdims=True)
            context = dot32(low(weight), values) * (1.0 / total)
            log_total = jnp.broadcast_to(top + jnp.log2(total), (step, 128))
            if head == 0:
                both, both_total = context, log_total
            else:
                both, both_total = jnp.where(mine, context, both), jnp.where(mine, log_total, both_total)
        out_ref[0, at : at + step, :] = low(both)
        turned = both_total.T
        total_ref[0, 0, 0:1, at : at + step] = turned[0:1]
        total_ref[0, 0, 1:2, at : at + step] = turned[64:65]


def attend(lengths, queries, keys, values, step, causal):
    tables, rows, width = queries.shape
    count = keys.shape[1]
    pair = lambda size: pl.BlockSpec((1, size, 128), lambda t, h, n: (t, 0, h))
    return pl.pallas_call(
        functools.partial(attend_kernel, step=step, causal=causal),
        grid_spec=pltpu.PrefetchScalarGridSpec(
            num_scalar_prefetch=1,
            grid=(tables, width // 128),
            in_specs=[pair(rows), pair(count), pair(count)],
            out_specs=[pair(rows), pl.BlockSpec((1, 1, 2, rows), lambda t, h, n: (t, h, 0, 0))],
        ),
        out_shape=[
            jax.ShapeDtypeStruct(queries.shape, jnp.bfloat16),
            jax.ShapeDtypeStruct((tables, width // 128, 2, rows), jnp.float32),
        ],
        compiler_params=pltpu.CompilerParams(vmem_limit_bytes=50 * 2**20),
        cost_estimate=pl.CostEstimate(
            flops=4 * tables * rows * count * width * 4,
            bytes_accessed=4 * tables * (rows + count) * width,
            transcendentals=tables * rows * count * width // 64,
        ),
        name="attend",
    )(lengths, queries, keys, values)


def attend_back_kernel(
    length, q_ref, k_ref, v_ref, grad_ref, out_ref, total_ref, dq_ref, dk_ref, dv_ref, *, step, causal
):
    valid = length[pl.program_id(0)]
    product = grad_ref[0].astype(jnp.float32) * out_ref[0].astype(jnp.float32)
    select = (
        lax.broadcasted_iota(jnp.int32, (8, 128), 1) // 64 == lax.broadcasted_iota(jnp.int32, (8, 128), 0)
    ).astype(jnp.float32)
    inner = lax.dot_general(
        select, product, NT, preferred_element_type=jnp.float32, precision=lax.Precision.HIGHEST
    )
    total_dq = None
    for at in range(0, k_ref.shape[1], step):
        first = at if causal else 0
        keys, values = k_ref[0, at : at + step, :], v_ref[0, at : at + step, :]
        queries, grads = q_ref[0, first:, :], grad_ref[0, first:, :]
        row = lax.broadcasted_iota(jnp.int32, (step, 1), 0)
        bias = jnp.where(row + at < valid, 0.0, MASKED).astype(jnp.float32)
        part_dq = None
        for head in range(2):
            mine = head_of_pair(step, head)
            own_keys = jnp.where(mine, keys, jnp.zeros_like(keys))
            own_values = jnp.where(mine, values, jnp.zeros_like(values))
            scores = dot32(own_keys, queries, NT) + bias
            if causal:
                key_at = lax.broadcasted_iota(jnp.int32, scores.shape, 0)
                scores = jnp.where(
                    key_at <= lax.broadcasted_iota(jnp.int32, scores.shape, 1), scores, MASKED
                )
            probs = jnp.exp2(scores - total_ref[0, 0, head : head + 1, first:])
            grad_probs = dot32(own_values, grads, NT)
            own_dv = dot32(low(probs), grads)
            grad_scores = low(probs * (grad_probs - inner[head : head + 1, first:]))
            own_dk = dot32(grad_scores, queries)
            own_dq = dot32(grad_scores, own_keys, TN)
            if head == 0:
                dk, dv, part_dq = own_dk, own_dv, own_dq
            else:
                dk, dv, part_dq = jnp.where(mine, own_dk, dk), jnp.where(mine, own_dv, dv), part_dq + own_dq
        dk_ref[0, at : at + step, :] = low(dk * LN2)
        dv_ref[0, at : at + step, :] = low(dv)
        if total_dq is None:
            total_dq = part_dq
        elif first == 0:
            total_dq = total_dq + part_dq
        else:
            total_dq = jnp.concatenate([total_dq[:first], total_dq[first:] + part_dq], axis=0)
    dq_ref[0] = low(total_dq * 0.125)


def attend_back(lengths, queries, keys, values, grads, out, log_total, step, causal):
    tables, rows, width = queries.shape
    count = keys.shape[1]
    pair = lambda size: pl.BlockSpec((1, size, 128), lambda t, h, n: (t, 0, h))
    return pl.pallas_call(
        functools.partial(attend_back_kernel, step=step, causal=causal),
        grid_spec=pltpu.PrefetchScalarGridSpec(
            num_scalar_prefetch=1,
            grid=(tables, width // 128),
            in_specs=[
                pair(rows), pair(count), pair(count), pair(rows), pair(rows),
                pl.BlockSpec((1, 1, 2, rows), lambda t, h, n: (t, h, 0, 0)),
            ],
            out_specs=[pair(rows), pair(count), pair(count)],
        ),
        out_shape=[
            jax.ShapeDtypeStruct(queries.shape, jnp.bfloat16),
            jax.ShapeDtypeStruct(keys.shape, jnp.bfloat16),
            jax.ShapeDtypeStruct(keys.shape, jnp.bfloat16),
        ],
        compiler_params=pltpu.CompilerParams(vmem_limit_bytes=50 * 2**20),
        cost_estimate=pl.CostEstimate(
            flops=10 * tables * rows * count * width * 4,
            bytes_accessed=4 * tables * (2 * rows + 2 * count) * width,
            transcendentals=tables * rows * count * width // 64,
        ),
        name="attend_back",
    )(lengths, queries, keys, values, grads, out, log_total)


def swap_seq(value):
    return lax.ppermute(value, "seq", [(0, 1), (1, 0)])


def swap_items(value, bit):
    count = lax.axis_size("items")
    return lax.ppermute(value, "items", [(at, at ^ bit) for at in range(count)])


def add_low(former, latter):
    return low(former.astype(jnp.float32) + latter.astype(jnp.float32))


def halve(parts, axis, bit, swap):
    keep = lax.dynamic_index_in_dim(parts, bit, axis, keepdims=False)
    away = lax.dynamic_index_in_dim(parts, 1 - bit, axis, keepdims=False)
    return add_low(keep, swap(away))


def norm_back(incoming, normal, root, gain_row):
    scaled = incoming * gain_row
    return root * (
        scaled
        - jnp.mean(scaled, axis=-1, keepdims=True)
        - normal * jnp.mean(scaled * normal, axis=-1, keepdims=True)
    )


def norm_parts(hidden):
    centre = hidden - jnp.mean(hidden, axis=-1, keepdims=True)
    root = lax.rsqrt(jnp.mean(centre * centre, axis=-1, keepdims=True) + 1e-05)
    return centre * root, root


def total32(value):
    return jnp.sum(value.astype(jnp.float32), axis=0)


def on_device_tables(
    target_in,
    memory,
    cotangent,
    target_len,
    memory_len,
    attn_in,
    attn_out,
    biases,
    norm_gain,
    norm_bias,
    up_weight,
    up_bias,
    down_weight,
):
    place = lax.axis_index("seq")
    item = lax.axis_index("items")
    core, y_at, z_low, z_high = item & 1, (item >> 1) & 1, (item >> 2) & 1, (item >> 3) & 1
    tables = target_in.shape[0] // 2
    model_width = target_in.shape[2]
    half_hidden = up_weight.shape[1]

    def gather_rows(value):
        away = lax.dynamic_slice_in_dim(value, (1 - place) * tables, tables, 0)
        own = lax.dynamic_slice_in_dim(value, place * tables, tables, 0)
        came = swap_seq(away)
        return jnp.where(
            place == 0, jnp.concatenate([own, came], 1), jnp.concatenate([came, own], 1)
        )

    def return_rows(value):
        half = value.shape[1] // 2
        away = low(lax.dynamic_slice_in_dim(value, (1 - place) * half, half, 1))
        own = lax.dynamic_slice_in_dim(value, place * half, half, 1)
        came = swap_seq(away).astype(own.dtype)
        return jnp.where(
            place == 0, jnp.concatenate([own, came], 0), jnp.concatenate([came, own], 0)
        )

    target = gather_rows(target_in)
    rows = target.shape[1]
    target_rows = target.reshape(-1, model_width)
    slices = model_width // lax.axis_size("items")
    sent = swap_seq(
        jnp.concatenate(
            [
                lax.dynamic_slice_in_dim(up_weight, item * slices, slices, 0),
                lax.dynamic_slice_in_dim(down_weight, item * slices, slices, 0),
            ],
            0,
        )
    )
    up_other = lax.all_gather(sent[:slices], "items", axis=0, tiled=True)
    down_other = lax.all_gather(sent[slices:], "items", axis=0, tiled=True)
    up_bias_other = swap_seq(up_bias)
    memory_full = gather_rows(memory)
    count = memory_full.shape[1]
    memory_rows = memory_full.reshape(-1, model_width)
    cotangent_rows = gather_rows(cotangent).reshape(-1, model_width)
    target_lengths = lax.dynamic_slice_in_dim(target_len[0], place * tables, tables, 0)
    memory_lengths = lax.dynamic_slice_in_dim(memory_len[0], place * tables, tables, 0)

    by_table = lambda value: value.reshape(tables, -1, model_width)
    flat = lambda value: value.reshape(-1, model_width)
    scale = 0.125 * LOG2E
    self_query = low((dot32(target_rows, attn_in[0]) + biases[0]) * scale)
    self_keys = low(dot32(target_rows, attn_in[1]))
    self_values = low(dot32(target_rows, attn_in[2]) + biases[1])
    self_context, self_total = attend(
        target_lengths, by_table(self_query), by_table(self_keys), by_table(self_values), rows, True
    )
    hidden_one = target_rows.astype(jnp.float32) + (dot32(flat(self_context), attn_out[0]) + biases[2])
    normal_one, root_one = norm_parts(hidden_one)
    norm_one = normal_one * norm_gain[0] + norm_bias[0]
    norm_one_low = low(norm_one)
    cross_query = low((dot32(norm_one_low, attn_in[3]) + biases[3]) * scale)
    cross_keys = low(dot32(memory_rows, attn_in[4]))
    cross_values = low(dot32(memory_rows, attn_in[5]) + biases[4])
    cross_context, cross_total = attend(
        memory_lengths, by_table(cross_query), by_table(cross_keys), by_table(cross_values), rows // 2, False
    )
    hidden_two = norm_one + (dot32(flat(cross_context), attn_out[1]) + biases[5])
    normal_two, root_two = norm_parts(hidden_two)
    norm_two = normal_two * norm_gain[1] + norm_bias[1]
    norm_two_low = low(norm_two)

    ffn_sum = 0.0
    halves = []
    for up_half, up_bias_half, down_half in (
        (up_weight, up_bias, down_weight),
        (up_other, up_bias_other, down_other),
    ):
        act = dot32(norm_two_low, up_half) + up_bias_half
        cdf = 0.5 * lax.erfc(act * -0.7071067811865476)
        up_out = low(act * cdf)
        slope = cdf + act * (0.3989422804014327 * jnp.exp(-0.5 * act * act))
        ffn_sum = ffn_sum + dot32(up_out, down_half, NT)
        halves.append((up_half, down_half, up_out, slope))
    hidden_three = norm_two + (ffn_sum + biases[6])
    normal_three, root_three = norm_parts(hidden_three)
    layer_rows = low(normal_three * norm_gain[2] + norm_bias[2])
    layer_out = return_rows(by_table(layer_rows))
    incoming = cotangent_rows.astype(jnp.float32)
    gain_three, shift_three = jnp.sum(incoming * normal_three, 0), jnp.sum(incoming, 0)
    grad_three = norm_back(incoming, normal_three, root_three, norm_gain[2])
    grad_ffn_out = low(grad_three)
    grad_norm_two = grad_three
    grad_acts = []
    for up_half, down_half, up_out, slope in halves:
        grad_act = low(dot32(grad_ffn_out, down_half) * slope)
        grad_norm_two = grad_norm_two + dot32(grad_act, up_half, NT)
        grad_acts.append(grad_act)
    by_holder = lambda value: value.reshape(-1, 2, 2, 2, 2, slices).transpose(4, 0, 3, 2, 1, 5).reshape(
        2, -1, model_width // 2
    )

    def ffn_outer(left, mine, other):
        left = by_holder(left)
        pick = lambda bit: lax.dynamic_index_in_dim(left, bit, 0, keepdims=False)
        away_left, keep_left = pick(1 - core), pick(core)
        away = jnp.concatenate([low(dot32(away_left, mine, TN)), low(dot32(away_left, other, TN))], 1)
        came = swap_items(away, 1)
        keep = jnp.concatenate(
            [
                low(dot32(keep_left, mine, TN) + came[:, :half_hidden].astype(jnp.float32)),
                low(dot32(keep_left, other, TN) + came[:, half_hidden:].astype(jnp.float32)),
            ],
            1,
        )
        keep = halve(keep.reshape(2, 4 * slices, 2 * half_hidden), 0, y_at, lambda v: swap_items(v, 2))
        keep = halve(keep.reshape(2, 2 * slices, 2 * half_hidden), 0, z_low, lambda v: swap_items(v, 4))
        keep = add_low(keep[:, :half_hidden], swap_seq(keep[:, half_hidden:]))
        keep = keep.reshape(2, slices, half_hidden)
        own = lax.dynamic_index_in_dim(keep, z_high, 0, keepdims=False)
        away = lax.dynamic_index_in_dim(keep, 1 - z_high, 0, keepdims=False)
        return own.astype(jnp.float32) + swap_items(away, 8).astype(jnp.float32)

    up_grad = ffn_outer(norm_two_low, *grad_acts)
    down_grad = ffn_outer(grad_ffn_out, halves[0][2], halves[1][2])
    up_bias_mine, up_bias_rest = total32(grad_acts[0]), total32(grad_acts[1])
    gain_two, shift_two = jnp.sum(grad_norm_two * normal_two, 0), jnp.sum(grad_norm_two, 0)
    grad_two = norm_back(grad_norm_two, normal_two, root_two, norm_gain[1])
    grad_cross_out = low(grad_two)
    grad_cross_context = low(dot32(grad_cross_out, attn_out[1], NT))
    grad_cross_query, grad_cross_keys, grad_cross_values = attend_back(
        memory_lengths,
        by_table(cross_query), by_table(cross_keys), by_table(cross_values),
        by_table(grad_cross_context), cross_context, cross_total, rows // 2, False,
    )
    grad_cross_query, grad_cross_keys, grad_cross_values = (
        flat(grad_cross_query), flat(grad_cross_keys), flat(grad_cross_values)
    )

    def attn_outer(pairs, last):
        inner = jnp.concatenate([low(dot32(left, right, TN)) for left, right in pairs], 0)
        outer = low(dot32(last[0], last[1], TN))
        parts = jnp.concatenate(
            [inner.reshape(16, -1, model_width), outer.reshape(16, -1, model_width)], 1
        ).reshape(2, 2, 2, 2, -1, model_width)
        parts = halve(parts, 2, core, lambda v: swap_items(v, 1))
        parts = halve(parts, 0, z_low, lambda v: swap_items(v, 4))
        parts = halve(parts, 0, y_at, lambda v: swap_items(v, 2))
        return halve(parts, 0, place, swap_seq)

    cross_part = attn_outer(
        [(norm_one_low, grad_cross_query), (memory_rows, grad_cross_keys), (memory_rows, grad_cross_values)],
        (flat(cross_context), grad_cross_out),
    )
    memory_grad = return_rows(
        by_table(dot32(grad_cross_keys, attn_in[4], NT) + dot32(grad_cross_values, attn_in[5], NT))
    )
    grad_norm_one = grad_two + dot32(grad_cross_query, attn_in[3], NT)
    gain_one, shift_one = jnp.sum(grad_norm_one * normal_one, 0), jnp.sum(grad_norm_one, 0)
    grad_one = norm_back(grad_norm_one, normal_one, root_one, norm_gain[0])
    grad_self_out = low(grad_one)
    grad_self_context = low(dot32(grad_self_out, attn_out[0], NT))
    grad_self_query, grad_self_keys, grad_self_values = attend_back(
        target_lengths,
        by_table(self_query), by_table(self_keys), by_table(self_values),
        by_table(grad_self_context), self_context, self_total, rows // 2, True,
    )
    grad_self_query, grad_self_keys, grad_self_values = (
        flat(grad_self_query), flat(grad_self_keys), flat(grad_self_values)
    )
    self_part = attn_outer(
        [(target_rows, grad_self_query), (target_rows, grad_self_keys), (target_rows, grad_self_values)],
        (flat(self_context), grad_self_out),
    )
    target_grad = return_rows(
        by_table(
            grad_one
            + dot32(grad_self_query, attn_in[0], NT)
            + dot32(grad_self_keys, attn_in[1], NT)
            + dot32(grad_self_values, attn_in[2], NT)
        )
    )
    own = jnp.where(z_high == 1, cross_part, self_part)
    away = jnp.where(z_high == 1, self_part, cross_part)
    shard = own.astype(jnp.float32) + swap_items(away, 8).astype(jnp.float32)
    inner_rows = 6 * model_width // (2 * lax.axis_size("items"))
    attn_in_grad, attn_out_grad = shard[:inner_rows], shard[inner_rows:]

    up_bias_total = jnp.where(
        place == 0,
        jnp.concatenate([up_bias_mine, up_bias_rest]),
        jnp.concatenate([up_bias_rest, up_bias_mine]),
    )
    small = jnp.concatenate(
        [
            jnp.stack(
                [
                    total32(grad_self_query), total32(grad_self_values), total32(grad_self_out),
                    total32(grad_cross_query), total32(grad_cross_values), total32(grad_cross_out),
                    total32(grad_ffn_out),
                    gain_one, gain_two, gain_three, shift_one, shift_two, shift_three,
                ]
            ),
            up_bias_total.reshape(-1, model_width),
        ],
        0,
    )
    for bit in (1, 2, 4, 8):
        small = small + swap_items(small, bit)
    small = small + swap_seq(small)
    return (
        layer_out,
        target_grad,
        memory_grad,
        attn_in_grad,
        attn_out_grad,
        small[:7],
        small[7:10],
        small[10:13],
        up_grad,
        small[13:].reshape(-1),
        down_grad,
    )


def solution(mesh):
    in_specs = (
        P("items", "seq", None),
        P("items", "seq", None),
        P("items", "seq", None),
        P("items", None),
        P("items", None),
        P(),
        P(),
        P(),
        P(),
        P(),
        P(None, "seq"),
        P("seq"),
        P(None, "seq"),
    )
    out_specs = (
        P("items", "seq", None),
        P("items", "seq", None),
        P("items", "seq", None),
        P(("items", "seq"), None),
        P(("items", "seq"), None),
        P(),
        P(),
        P(),
        P("items", "seq"),
        P(),
        P("items", "seq"),
    )
    whole_tables = mesh.shape["seq"] == 2 and mesh.shape["items"] == 16
    plan = on_device_tables if whole_tables else on_device
    return jax.shard_map(
        plan, mesh=mesh, in_specs=in_specs, out_specs=out_specs, check_vma=False
    )
```

```python
import functools
import math

import jax
import jax.numpy as jnp
from jax import lax
from jax.experimental import pallas as pl
from jax.experimental.pallas import tpu as pltpu
from jax.sharding import PartitionSpec as P

H = 16


def layer_norm(hidden, gain_row, shift_row):
    centre = hidden - jnp.mean(hidden, axis=-1, keepdims=True)
    spread = jnp.mean(centre * centre, axis=-1, keepdims=True)
    return centre * lax.rsqrt(spread + 1e-05) * gain_row + shift_row


def gelu_exact(argument):
    return jax.nn.gelu(argument, approximate=False)


def project(hidden_rows, weight):
    return jnp.einsum("tld,de->tle", hidden_rows, weight, preferred_element_type=jnp.float32)


def project_back(gradient, weight):
    return jnp.einsum("tle,de->tld", gradient, weight, preferred_element_type=jnp.float32)


def exact_back(gradient, weight):
    return jnp.einsum(
        "tle,de->tld", gradient, weight.astype(jnp.float32), precision=lax.Precision.HIGHEST
    )


def outer_sum(former, latter):
    return jnp.einsum("tld,tle->de", former, latter, preferred_element_type=jnp.float32)


def exact_outer(former, latter):
    return jnp.einsum(
        "tld,tle->de", former.astype(jnp.float32), latter, precision=lax.Precision.HIGHEST
    )


def column_total(gradient):
    return jnp.sum(gradient.astype(jnp.float32), axis=(0, 1))


def split_heads(hidden_rows):
    return hidden_rows.reshape(
        hidden_rows.shape[0], hidden_rows.shape[1], H, hidden_rows.shape[2] // H
    )


def attn_scores(queries, key_rows, allowed):
    score_scale = 1.0 / math.sqrt(queries.shape[2] // H)
    scores = (
        jnp.einsum(
            "tqhe,tkhe->thqk",
            split_heads(queries),
            split_heads(key_rows),
            preferred_element_type=jnp.float32,
        )
        * score_scale
    )
    return jnp.where(allowed[:, None], scores, -1e30)


def attn_forward(queries, key_rows, value_rows, allowed):
    scores = attn_scores(queries, key_rows, allowed)
    row_top = jnp.max(scores, axis=-1, keepdims=True)
    exponent = jnp.exp(scores - row_top)
    row_total = jnp.sum(exponent, axis=-1, keepdims=True)
    probability = exponent / row_total
    context = jnp.einsum(
        "thqk,tkhe->tqhe",
        probability.astype(jnp.bfloat16),
        split_heads(value_rows),
        preferred_element_type=jnp.float32,
    )
    return (context.reshape(queries.shape).astype(jnp.bfloat16), row_top + jnp.log(row_total))


def attn_backward(queries, key_rows, value_rows, allowed, log_total, grad_context):
    score_scale = 1.0 / math.sqrt(queries.shape[2] // H)
    scores = attn_scores(queries, key_rows, allowed)
    probability = jnp.exp(scores - log_total)
    grad_heads = split_heads(grad_context)
    grad_values = jnp.einsum(
        "thqk,tqhe->tkhe",
        probability.astype(jnp.bfloat16),
        grad_heads,
        preferred_element_type=jnp.float32,
    )
    grad_probs = jnp.einsum(
        "tqhe,tkhe->thqk", grad_heads, split_heads(value_rows), preferred_element_type=jnp.float32
    )
    grad_scores = probability * (
        grad_probs - jnp.sum(probability * grad_probs, axis=-1, keepdims=True)
    )
    grad_scores = grad_scores.astype(jnp.bfloat16)
    grad_query = (
        jnp.einsum(
            "thqk,tkhe->tqhe",
            grad_scores,
            split_heads(key_rows),
            preferred_element_type=jnp.float32,
        )
        * score_scale
    )
    grad_keys = (
        jnp.einsum(
            "thqk,tqhe->tkhe", grad_scores, split_heads(queries), preferred_element_type=jnp.float32
        )
        * score_scale
    )
    return (
        grad_query.reshape(queries.shape).astype(jnp.bfloat16),
        grad_keys.reshape(key_rows.shape),
        grad_values.reshape(value_rows.shape),
    )


def on_device(
    target_in,
    memory,
    cotangent,
    target_len,
    memory_len,
    attn_in,
    attn_out,
    biases,
    norm_gain,
    norm_bias,
    up_weight,
    up_bias,
    down_weight,
):
    seq_count = lax.axis_size("seq")
    seq_place = lax.axis_index("seq")
    local_rows = target_in.shape[1]
    model_width = target_in.shape[2]
    full_rows = local_rows * seq_count
    memory_full = memory.shape[1] * seq_count
    hidden_local = up_weight.shape[1]
    target_length = target_len[0]
    memory_length = memory_len[0]
    query_place = seq_place * local_rows + jnp.arange(local_rows, dtype=jnp.int32)
    key_place = jnp.arange(full_rows, dtype=jnp.int32)
    causal = (key_place[None, None, :] <= query_place[None, :, None]) & (
        key_place[None, None, :] < target_length[:, None, None]
    )
    visible = jnp.arange(memory_full, dtype=jnp.int32)[None, None, :] < memory_length[:, None, None]
    self_query = (project(target_in, attn_in[0]) + biases[0]).astype(jnp.bfloat16)
    self_keys = project(target_in, attn_in[1]).astype(jnp.bfloat16)
    self_values = (project(target_in, attn_in[2]) + biases[1]).astype(jnp.bfloat16)
    all_keys, all_values = (
        lax.all_gather(self_keys, "seq", axis=1, tiled=True),
        lax.all_gather(self_values, "seq", axis=1, tiled=True),
    )
    self_context, self_total = attn_forward(self_query, all_keys, all_values, causal)
    hidden_one = target_in.astype(jnp.float32) + (project(self_context, attn_out[0]) + biases[2])
    norm_one = layer_norm(hidden_one, norm_gain[0], norm_bias[0])
    norm_one_low = norm_one.astype(jnp.bfloat16)
    cross_query = (project(norm_one_low, attn_in[3]) + biases[3]).astype(jnp.bfloat16)
    local_keys = project(memory, attn_in[4]).astype(jnp.bfloat16)
    local_values = (project(memory, attn_in[5]) + biases[4]).astype(jnp.bfloat16)
    cross_keys, cross_values = (
        lax.all_gather(local_keys, "seq", axis=1, tiled=True),
        lax.all_gather(local_values, "seq", axis=1, tiled=True),
    )
    cross_context, cross_total = attn_forward(cross_query, cross_keys, cross_values, visible)
    hidden_two = norm_one + (project(cross_context, attn_out[1]) + biases[5])
    norm_two = layer_norm(hidden_two, norm_gain[1], norm_bias[1])
    ffn_rows = lax.all_gather(norm_two.astype(jnp.bfloat16), "seq", axis=1, tiled=True)
    up_act = project(ffn_rows, up_weight) + up_bias
    up_out = gelu_exact(up_act).astype(jnp.bfloat16)
    ffn_sum = lax.psum_scatter(
        project_back(up_out, down_weight), "seq", scatter_dimension=1, tiled=True
    )
    hidden_three = norm_two + (ffn_sum + biases[6])
    final_rows, pull_three = jax.vjp(layer_norm, hidden_three, norm_gain[2], norm_bias[2])
    layer_out = final_rows.astype(jnp.bfloat16)
    grad_three, gain_three, shift_three = pull_three(cotangent.astype(jnp.float32))
    grad_ffn_out = grad_three.astype(jnp.bfloat16)
    grad_ffn_rows = lax.all_gather(grad_ffn_out, "seq", axis=1, tiled=True)
    grad_up_out = project(grad_ffn_rows, down_weight)
    unused_act, pull_gelu = jax.vjp(gelu_exact, up_act)
    grad_up_act = pull_gelu(grad_up_out)[0].astype(jnp.bfloat16)
    down_local = outer_sum(grad_ffn_rows, up_out)
    up_local = outer_sum(ffn_rows, grad_up_act)
    up_bias_local = column_total(grad_up_act)
    grad_norm_two = grad_three + lax.psum_scatter(
        project_back(grad_up_act, up_weight), "seq", scatter_dimension=1, tiled=True
    )
    unused_two, pull_two = jax.vjp(layer_norm, hidden_two, norm_gain[1], norm_bias[1])
    grad_two, gain_two, shift_two = pull_two(grad_norm_two)
    grad_cross_out = grad_two.astype(jnp.bfloat16)
    grad_cross_context = project_back(grad_cross_out, attn_out[1]).astype(jnp.bfloat16)
    grad_cross_query, cross_key_part, cross_value_part = attn_backward(
        cross_query, cross_keys, cross_values, visible, cross_total, grad_cross_context
    )
    key_grad, value_grad = (
        lax.psum_scatter(
            cross_key_part.astype(jnp.bfloat16), "seq", scatter_dimension=1, tiled=True
        ).astype(jnp.float32),
        lax.psum_scatter(
            cross_value_part.astype(jnp.bfloat16), "seq", scatter_dimension=1, tiled=True
        ).astype(jnp.float32),
    )
    memory_grad = exact_back(key_grad, attn_in[4]) + exact_back(value_grad, attn_in[5])
    memory_key_outer = exact_outer(memory, key_grad)
    memory_value_outer = exact_outer(memory, value_grad)
    cross_value_total = column_total(value_grad)
    grad_norm_one = grad_two + project_back(grad_cross_query, attn_in[3])
    unused_one, pull_one = jax.vjp(layer_norm, hidden_one, norm_gain[0], norm_bias[0])
    grad_one, gain_one, shift_one = pull_one(grad_norm_one)
    grad_self_out = grad_one.astype(jnp.bfloat16)
    grad_self_context = project_back(grad_self_out, attn_out[0]).astype(jnp.bfloat16)
    grad_self_query, self_key_part, self_value_part = attn_backward(
        self_query, all_keys, all_values, causal, self_total, grad_self_context
    )
    self_key_grad, self_value_grad = (
        lax.psum_scatter(
            self_key_part.astype(jnp.bfloat16), "seq", scatter_dimension=1, tiled=True
        ).astype(jnp.float32),
        lax.psum_scatter(
            self_value_part.astype(jnp.bfloat16), "seq", scatter_dimension=1, tiled=True
        ).astype(jnp.float32),
    )
    target_kv = exact_back(self_key_grad, attn_in[1]) + exact_back(self_value_grad, attn_in[2])
    self_key_outer = exact_outer(target_in, self_key_grad)
    self_value_outer = exact_outer(target_in, self_value_grad)
    self_value_total = column_total(self_value_grad)
    target_grad = grad_one + project_back(grad_self_query, attn_in[0]) + target_kv
    inner_grads = jnp.stack(
        [
            outer_sum(target_in, grad_self_query),
            self_key_outer,
            self_value_outer,
            outer_sum(norm_one_low, grad_cross_query),
            memory_key_outer,
            memory_value_outer,
        ]
    )
    outer_grads = jnp.stack(
        [outer_sum(self_context, grad_self_out), outer_sum(cross_context, grad_cross_out)]
    )
    attn_in_grad, attn_out_grad = (
        lax.psum_scatter(
            inner_grads.reshape(6 * model_width, model_width),
            ("items", "seq"),
            scatter_dimension=0,
            tiled=True,
        ),
        lax.psum_scatter(
            outer_grads.reshape(2 * model_width, model_width),
            ("items", "seq"),
            scatter_dimension=0,
            tiled=True,
        ),
    )
    up_grad, down_grad = (
        lax.psum_scatter(
            up_local.astype(jnp.bfloat16), "items", scatter_dimension=0, tiled=True
        ).astype(jnp.float32),
        lax.psum_scatter(
            down_local.astype(jnp.bfloat16), "items", scatter_dimension=0, tiled=True
        ).astype(jnp.float32),
    )
    bias_local = jnp.stack(
        [
            column_total(grad_self_query),
            self_value_total,
            column_total(grad_self_out),
            column_total(grad_cross_query),
            cross_value_total,
            column_total(grad_cross_out),
            column_total(grad_ffn_out),
        ]
    )
    gain_local = jnp.stack([gain_one, gain_two, gain_three])
    shift_local = jnp.stack([shift_one, shift_two, shift_three])
    up_bias_full = lax.dynamic_update_slice(
        jnp.zeros((hidden_local * seq_count,), jnp.float32),
        up_bias_local,
        (seq_place * hidden_local,),
    )
    bias_grad, gain_grad, norm_bias_grad, up_bias_grad = lax.psum(
        (bias_local, gain_local, shift_local, up_bias_full), ("items", "seq")
    )
    return (
        layer_out,
        target_grad,
        memory_grad,
        attn_in_grad,
        attn_out_grad,
        bias_grad,
        gain_grad,
        norm_bias_grad,
        up_grad,
        up_bias_grad,
        down_grad,
    )


NT = (((1,), (1,)), ((), ()))
NN = (((1,), (0,)), ((), ()))
TN = (((0,), (0,)), ((), ()))
LOG2E = 1.4426950408889634
LN2 = 0.6931471805599453
MASKED = -1e30


def dot32(former, latter, dims=NN):
    return lax.dot_general(former, latter, dims, preferred_element_type=jnp.float32)


def low(value):
    return value.astype(jnp.bfloat16)


def head_of_pair(rows, head):
    return lax.broadcasted_iota(jnp.int32, (rows, 128), 1) // 64 == head


def attend_kernel(length, q_ref, k_ref, v_ref, out_ref, total_ref, *, step, causal):
    valid = length[pl.program_id(0)]
    for at in range(0, q_ref.shape[1], step):
        seen = at + step if causal else k_ref.shape[1]
        queries, keys, values = q_ref[0, at : at + step, :], k_ref[0, :seen, :], v_ref[0, :seen, :]
        column = lax.broadcasted_iota(jnp.int32, (1, seen), 1)
        bias = jnp.where(column < valid, 0.0, MASKED).astype(jnp.float32)
        if causal:
            row = lax.broadcasted_iota(jnp.int32, (step, seen), 0) + at
            order = lax.broadcasted_iota(jnp.int32, (step, seen), 1) <= row
        for head in range(2):
            mine = head_of_pair(step, head)
            scores = dot32(jnp.where(mine, queries, jnp.zeros_like(queries)), keys, NT) + bias
            if causal:
                scores = jnp.where(order, scores, MASKED)
            top = jnp.max(scores, axis=1, keepdims=True)
            weight = jnp.exp2(scores - top)
            total = jnp.sum(weight, axis=1, keepdims=True)
            context = dot32(low(weight), values) * (1.0 / total)
            log_total = jnp.broadcast_to(top + jnp.log2(total), (step, 128))
            if head == 0:
                both, both_total = context, log_total
            else:
                both, both_total = jnp.where(mine, context, both), jnp.where(mine, log_total, both_total)
        out_ref[0, at : at + step, :] = low(both)
        turned = both_total.T
        total_ref[0, 0, 0:1, at : at + step] = turned[0:1]
        total_ref[0, 0, 1:2, at : at + step] = turned[64:65]


def pair_of(index, size):
    return pl.BlockSpec((None, 1, size, 128), lambda t, h, n: (index, t, 0, h))


def attend(lengths, queries, keys, values, at, step, causal):
    _, tables, rows, width = queries.shape
    count = keys.shape[2]
    pair = lambda size: pl.BlockSpec((1, size, 128), lambda t, h, n: (t, 0, h))
    return pl.pallas_call(
        functools.partial(attend_kernel, step=step, causal=causal),
        grid_spec=pltpu.PrefetchScalarGridSpec(
            num_scalar_prefetch=1,
            grid=(tables, width // 128),
            in_specs=[pair_of(at[0], rows), pair_of(at[1], count), pair_of(at[2], count)],
            out_specs=[pair(rows), pl.BlockSpec((1, 1, 2, rows), lambda t, h, n: (t, h, 0, 0))],
        ),
        out_shape=[
            jax.ShapeDtypeStruct((tables, rows, width), jnp.bfloat16),
            jax.ShapeDtypeStruct((tables, width // 128, 2, rows), jnp.float32),
        ],
        compiler_params=pltpu.CompilerParams(vmem_limit_bytes=50 * 2**20),
        cost_estimate=pl.CostEstimate(
            flops=4 * tables * rows * count * width * 4,
            bytes_accessed=4 * tables * (rows + count) * width,
            transcendentals=tables * rows * count * width // 64,
        ),
        name="attend",
    )(lengths, queries, keys, values)


def attend_back_kernel(
    length, q_ref, k_ref, v_ref, grad_ref, out_ref, total_ref, dq_ref, dk_ref, dv_ref, *, step, causal
):
    valid = length[pl.program_id(0)]
    product = grad_ref[0].astype(jnp.float32) * out_ref[0].astype(jnp.float32)
    select = (
        lax.broadcasted_iota(jnp.int32, (8, 128), 1) // 64 == lax.broadcasted_iota(jnp.int32, (8, 128), 0)
    ).astype(jnp.float32)
    inner = lax.dot_general(
        select, product, NT, preferred_element_type=jnp.float32, precision=lax.Precision.HIGHEST
    )
    total_dq = None
    for at in range(0, k_ref.shape[1], step):
        first = at if causal else 0
        keys, values = k_ref[0, at : at + step, :], v_ref[0, at : at + step, :]
        queries, grads = q_ref[0, first:, :], grad_ref[0, first:, :]
        row = lax.broadcasted_iota(jnp.int32, (step, 1), 0)
        bias = jnp.where(row + at < valid, 0.0, MASKED).astype(jnp.float32)
        part_dq = None
        for head in range(2):
            mine = head_of_pair(step, head)
            own_keys = jnp.where(mine, keys, jnp.zeros_like(keys))
            own_values = jnp.where(mine, values, jnp.zeros_like(values))
            scores = dot32(own_keys, queries, NT) + bias
            if causal:
                key_at = lax.broadcasted_iota(jnp.int32, scores.shape, 0)
                scores = jnp.where(
                    key_at <= lax.broadcasted_iota(jnp.int32, scores.shape, 1), scores, MASKED
                )
            probs = jnp.exp2(scores - total_ref[0, 0, head : head + 1, first:])
            grad_probs = dot32(own_values, grads, NT)
            own_dv = dot32(low(probs), grads)
            grad_scores = low(probs * (grad_probs - inner[head : head + 1, first:]))
            own_dk = dot32(grad_scores, queries)
            own_dq = dot32(grad_scores, own_keys, TN)
            if head == 0:
                dk, dv, part_dq = own_dk, own_dv, own_dq
            else:
                dk, dv, part_dq = jnp.where(mine, own_dk, dk), jnp.where(mine, own_dv, dv), part_dq + own_dq
        dk_ref[0, at : at + step, :] = low(dk * LN2)
        dv_ref[0, at : at + step, :] = low(dv)
        if total_dq is None:
            total_dq = part_dq
        elif first == 0:
            total_dq = total_dq + part_dq
        else:
            total_dq = jnp.concatenate([total_dq[:first], total_dq[first:] + part_dq], axis=0)
    dq_ref[0] = low(total_dq * 0.125)


def attend_back(lengths, queries, keys, values, at, grads, out, log_total, step, causal):
    _, tables, rows, width = queries.shape
    count = keys.shape[2]
    pair = lambda size: pl.BlockSpec((1, size, 128), lambda t, h, n: (t, 0, h))
    return pl.pallas_call(
        functools.partial(attend_back_kernel, step=step, causal=causal),
        grid_spec=pltpu.PrefetchScalarGridSpec(
            num_scalar_prefetch=1,
            grid=(tables, width // 128),
            in_specs=[
                pair_of(at[0], rows), pair_of(at[1], count), pair_of(at[2], count), pair(rows), pair(rows),
                pl.BlockSpec((1, 1, 2, rows), lambda t, h, n: (t, h, 0, 0)),
            ],
            out_specs=[pair(rows), pair(count), pair(count)],
        ),
        out_shape=[
            jax.ShapeDtypeStruct((tables, rows, width), jnp.bfloat16),
            jax.ShapeDtypeStruct((tables, count, width), jnp.bfloat16),
            jax.ShapeDtypeStruct((tables, count, width), jnp.bfloat16),
        ],
        compiler_params=pltpu.CompilerParams(vmem_limit_bytes=50 * 2**20),
        cost_estimate=pl.CostEstimate(
            flops=10 * tables * rows * count * width * 4,
            bytes_accessed=4 * tables * (2 * rows + 2 * count) * width,
            transcendentals=tables * rows * count * width // 64,
        ),
        name="attend_back",
    )(lengths, queries, keys, values, grads, out, log_total)


def swap_seq(value):
    return lax.ppermute(value, "seq", [(0, 1), (1, 0)])


def swap_items(value, bit):
    count = lax.axis_size("items")
    return lax.ppermute(value, "items", [(at, at ^ bit) for at in range(count)])


def add_low(former, latter):
    return low(former.astype(jnp.float32) + latter.astype(jnp.float32))


def halve(parts, axis, bit, swap):
    keep = lax.dynamic_index_in_dim(parts, bit, axis, keepdims=False)
    away = lax.dynamic_index_in_dim(parts, 1 - bit, axis, keepdims=False)
    return add_low(keep, swap(away))


def norm_back(incoming, normal, root, gain_row):
    scaled = incoming * gain_row
    return root * (
        scaled
        - jnp.mean(scaled, axis=-1, keepdims=True)
        - normal * jnp.mean(scaled * normal, axis=-1, keepdims=True)
    )


def norm_parts(hidden):
    centre = hidden - jnp.mean(hidden, axis=-1, keepdims=True)
    root = lax.rsqrt(jnp.mean(centre * centre, axis=-1, keepdims=True) + 1e-05)
    return centre * root, root


def total32(value):
    return jnp.sum(value.astype(jnp.float32), axis=0)


VMEM_LIMIT = 56 * 2**20


def whole(shape):
    return pl.BlockSpec(shape, lambda *at: (0,) * len(shape), pipeline_mode=pl.Buffered(1))


def pick(index, shape):
    return pl.BlockSpec((1,) + shape, lambda *at: (index,) + (0,) * len(shape), pipeline_mode=pl.Buffered(1))


def rows_of(size, width):
    return pl.BlockSpec((size, width), lambda at, *more: (at, 0))


def cost(flops, moved, transcendentals=0):
    return pl.CostEstimate(flops=int(flops), bytes_accessed=int(moved), transcendentals=int(transcendentals))


def add_rows(ref, at, value):
    ref[at : at + 1, :] += jnp.sum(value, axis=0, keepdims=True)


def project_kernel(place_ref, own_ref, came_ref, w_ref, bias_ref, scale_ref, out_ref, rows_ref):
    tables, half, width = own_ref.shape
    source, matrix = pl.program_id(0), pl.program_id(1)

    def run(ref):
        @pl.when(matrix == 0)
        def _():
            rows_ref[:, 0] = ref[...]

        value = dot32(ref[...].reshape(tables * half, width), w_ref[0])
        out_ref[0, :, 0] = low((value + bias_ref[0]) * scale_ref[0]).reshape(tables, half, width)

    pl.when(source == 0)(lambda: run(own_ref))
    pl.when(source == 1)(lambda: run(came_ref))


def project_halves(place, own, came, weights, first, bias, scale):
    tables, half, width = own.shape
    number = bias.shape[0]
    vector = pl.BlockSpec((1, 1, width), lambda s, k, p: (k, 0, 0))
    projected, rows = pl.pallas_call(
        project_kernel,
        grid_spec=pltpu.PrefetchScalarGridSpec(
            num_scalar_prefetch=1,
            grid=(2, number),
            in_specs=[
                whole(own.shape), whole(came.shape),
                pl.BlockSpec((1, width, width), lambda s, k, p: (first + k, 0, 0)), vector, vector,
            ],
            out_specs=[
                pl.BlockSpec((1, tables, 1, half, width), lambda s, k, p: (k, 0, s ^ p[0], 0, 0)),
                pl.BlockSpec((tables, 1, half, width), lambda s, k, p: (0, s ^ p[0], 0, 0)),
            ],
        ),
        out_shape=[
            jax.ShapeDtypeStruct((number, tables, 2, half, width), jnp.bfloat16),
            jax.ShapeDtypeStruct((tables, 2, half, width), jnp.bfloat16),
        ],
        compiler_params=pltpu.CompilerParams(vmem_limit_bytes=VMEM_LIMIT),
        cost_estimate=cost(
            4 * number * tables * half * width * width, 4 * (number + 2) * tables * half * width + 4 * number * width * width
        ),
        name="project_halves",
    )(place.reshape(1), own, came, weights, bias[:, None], scale[:, None])
    return projected.reshape(number, tables, 2 * half, width), rows.reshape(2 * tables * half, width)


def mix_kernel(ctx_ref, x_ref, wo_ref, wq_ref, bias_ref, gain_ref, shift_ref, n_ref, r_ref, low_ref, q_ref):
    hidden = x_ref[...].astype(jnp.float32) + (dot32(ctx_ref[...], wo_ref[0]) + bias_ref[2:3])
    normal, root = norm_parts(hidden)
    n_ref[...] = normal
    r_ref[...] = root
    normed = low(normal * gain_ref[0:1] + shift_ref[0:1])
    low_ref[...] = normed
    q_ref[...] = low((dot32(normed, wq_ref[0]) + bias_ref[3:4]) * (0.125 * LOG2E))


def mix(context, rows, attn_out, attn_in, biases, gain, shift, step):
    count, width = rows.shape
    block = rows_of(step, width)
    return pl.pallas_call(
        mix_kernel,
        grid=(count // step,),
        in_specs=[
            block, block, pick(0, (width, width)), pick(3, (width, width)),
            whole(biases.shape), whole(gain.shape), whole(shift.shape),
        ],
        out_specs=[block, rows_of(step, 1), block, block],
        out_shape=[
            jax.ShapeDtypeStruct((count, width), jnp.float32),
            jax.ShapeDtypeStruct((count, 1), jnp.float32),
            jax.ShapeDtypeStruct((count, width), jnp.bfloat16),
            jax.ShapeDtypeStruct((count, width), jnp.bfloat16),
        ],
        compiler_params=pltpu.CompilerParams(vmem_limit_bytes=VMEM_LIMIT),
        cost_estimate=cost(4 * count * width * width, 14 * count * width + 4 * width * width),
        name="mix",
    )(context, rows, attn_out, attn_in, biases, gain, shift)


def ffn_kernel(
    place_ref, ctx_ref, n1_ref, cot_own, cot_came, wo_all, up_a_all, up_b_all, down_a_all, down_b_all, ub_a, ub_b,
    bias_ref, gain_ref, shift_ref,
    own_ref, away_ref, right_ref, left_ref, gtwo_ref, gco_ref, gcc_ref, sums_ref, ubs_ref,
    slope_ref, wo_ref, up_a, down_a, up_b, down_b, arrived, *, chunk,
):
    first = pl.program_id(0) == 0
    mine = pl.program_id(0) % 2 == place_ref[0]
    copies = [
        pltpu.make_async_copy(source, target, arrived.at[at])
        for at, (source, target) in enumerate(
            (
                (wo_all.at[1], wo_ref), (up_a_all, up_a), (down_a_all, down_a), (up_b_all, up_b), (down_b_all, down_b)
            )
        )
    ]

    def need(at):
        @pl.when(first)
        def _():
            copies[at].wait()

    @pl.when(first)
    def _():
        for copy in copies:
            copy.start()
        sums_ref[...] = jnp.zeros_like(sums_ref)
        ubs_ref[...] = jnp.zeros_like(ubs_ref)

    half = up_a.shape[1]
    norm_one = n1_ref[...] * gain_ref[0:1] + shift_ref[0:1]
    need(0)
    normal_two, root_two = norm_parts(norm_one + (dot32(ctx_ref[...], wo_ref[...]) + bias_ref[5:6]))
    norm_two = normal_two * gain_ref[1:2] + shift_ref[1:2]
    normed = low(norm_two)
    left_ref[0] = normed
    total = norm_two + bias_ref[6:7]
    for side, (up, down, ub) in enumerate(((up_a, down_a, ub_a), (up_b, down_b, ub_b))):
        need(1 + 2 * side)
        need(2 + 2 * side)
        for at in range(0, half, chunk):
            act = dot32(normed, up[:, at : at + chunk]) + ub[:, at : at + chunk]
            cdf = 0.5 + 0.5 * lax.erf(act * 0.7071067811865476)
            slope = cdf + act * (0.3989422804014327 * jnp.exp(act * act * -0.5))
            hidden = low(act * cdf)
            place = side * half + at
            right_ref[1, :, place : place + chunk] = hidden
            slope_ref[:, place : place + chunk] = slope
            total = total + dot32(hidden, down[:, at : at + chunk], NT)
    normal_three, root_three = norm_parts(total)
    layer = low(normal_three * gain_ref[2:3] + shift_ref[2:3])

    @pl.when(mine)
    def _():
        own_ref[0] = layer

    @pl.when(jnp.logical_not(mine))
    def _():
        away_ref[0] = layer

    incoming = jnp.where(mine, cot_own[0], cot_came[0]).astype(jnp.float32)
    add_rows(sums_ref, 0, incoming * normal_three)
    add_rows(sums_ref, 1, incoming)
    grad_three = norm_back(incoming, normal_three, root_three, gain_ref[2:3])
    grad_ffn = low(grad_three)
    left_ref[1] = grad_ffn
    add_rows(sums_ref, 2, grad_ffn.astype(jnp.float32))
    total = grad_three
    for side, (up, down) in enumerate(((up_a, down_a), (up_b, down_b))):
        for at in range(0, half, chunk):
            place = side * half + at
            grad = low(dot32(grad_ffn, down[:, at : at + chunk]) * slope_ref[:, place : place + chunk])
            right_ref[0, :, place : place + chunk] = grad
            ubs_ref[:, place : place + chunk] += jnp.sum(grad.astype(jnp.float32), axis=0, keepdims=True)
            total = total + dot32(grad, up[:, at : at + chunk], NT)
    add_rows(sums_ref, 3, total * normal_two)
    add_rows(sums_ref, 4, total)
    grad_two = norm_back(total, normal_two, root_two, gain_ref[1:2])
    gtwo_ref[...] = grad_two
    rounded = low(grad_two)
    gco_ref[...] = rounded
    add_rows(sums_ref, 5, rounded.astype(jnp.float32))
    gcc_ref[...] = low(dot32(rounded, wo_ref[...], NT))


def ffn(
    place, context, normal_one, cot_own, cot_came, attn_out, up_a, up_b, down_a, down_b, ub_a, ub_b, biases, gain, shift, chunk
):
    count, width = context.shape
    tables, step, _ = cot_own.shape
    half = up_a.shape[1]
    block = pl.BlockSpec((step, width), lambda at, p: (at, 0))
    part = pl.BlockSpec((1, step, width), lambda at, p: (at // 2, 0, 0))
    stacked = lambda size: pl.BlockSpec((2, step, size), lambda at, p: (0, at, 0))
    low_rows = jax.ShapeDtypeStruct((count, width), jnp.bfloat16)
    outside = pl.BlockSpec(memory_space=pl.ANY)
    return pl.pallas_call(
        functools.partial(ffn_kernel, chunk=chunk),
        grid_spec=pltpu.PrefetchScalarGridSpec(
            num_scalar_prefetch=1,
            grid=(count // step,),
            in_specs=[block, block, part, part]
            + [outside] * 5
            + [whole((1, half)), whole((1, half)), whole(biases.shape), whole(gain.shape), whole(shift.shape)],
            out_specs=[
                pl.BlockSpec((1, step, width), lambda at, p: (p[0] * tables + at // 2, 0, 0)), part,
                stacked(2 * half), stacked(width), block, block, block, whole((8, width)), whole((1, 2 * half)),
            ],
            scratch_shapes=[
                pltpu.VMEM((step, 2 * half), jnp.float32),
                pltpu.VMEM((width, width), jnp.bfloat16),
                pltpu.VMEM((width, half), jnp.bfloat16),
                pltpu.VMEM((width, half), jnp.bfloat16),
                pltpu.VMEM((width, half), jnp.bfloat16),
                pltpu.VMEM((width, half), jnp.bfloat16),
                pltpu.SemaphoreType.DMA((5,)),
            ],
        ),
        out_shape=[
            jax.ShapeDtypeStruct((2 * tables, step, width), jnp.bfloat16),
            jax.ShapeDtypeStruct((tables, step, width), jnp.bfloat16),
            jax.ShapeDtypeStruct((2, count, 2 * half), jnp.bfloat16),
            jax.ShapeDtypeStruct((2, count, width), jnp.bfloat16),
            jax.ShapeDtypeStruct((count, width), jnp.float32), low_rows, low_rows,
            jax.ShapeDtypeStruct((8, width), jnp.float32),
            jax.ShapeDtypeStruct((1, 2 * half), jnp.float32),
        ],
        compiler_params=pltpu.CompilerParams(vmem_limit_bytes=VMEM_LIMIT),
        cost_estimate=cost((16 * half + 4 * width) * count * width, 40 * 2**20, 4 * count * half),
        name="ffn",
    )(
        place.reshape(1), context, normal_one, cot_own, cot_came, attn_out, up_a, up_b, down_a, down_b,
        ub_a[None], ub_b[None], biases, gain, shift,
    )


def ffn_outer_kernel(bit_ref, left_ref, right_ref, *refs):
    value = dot32(left_ref[...], right_ref[...], TN)
    if len(refs) == 2:
        value = value + refs[0][...].astype(jnp.float32)
    refs[-1][...] = low(value)


def ffn_outer(bit, left, right, at, came, step):
    _, count, width = left.shape
    total = right.shape[2]
    quarter = total // 4 // step
    column = pl.BlockSpec((width, step), lambda n, b: (0, n))
    extra = [] if came is None else [came]
    return pl.pallas_call(
        ffn_outer_kernel,
        grid_spec=pltpu.PrefetchScalarGridSpec(
            num_scalar_prefetch=1,
            grid=(2 * quarter,),
            in_specs=[
                pl.BlockSpec((None, count, width), lambda n, b: (at, 0, 0), pipeline_mode=pl.Buffered(1)),
                pl.BlockSpec(
                    (None, count, step), lambda n, b: (at, 0, (n // quarter * 2 + b[0]) * quarter + n % quarter)
                ),
            ]
            + [column] * len(extra),
            out_specs=column,
        ),
        out_shape=jax.ShapeDtypeStruct((width, total // 2), jnp.bfloat16),
        compiler_params=pltpu.CompilerParams(vmem_limit_bytes=VMEM_LIMIT),
        cost_estimate=cost(count * width * total, 2 * count * (width + total // 2) + 2 * width * total),
        name="ffn_outer",
    )(bit.reshape(1), left, right, *extra)


def group_outer_kernel(bit_ref, *refs, lefts, number, adds):
    distinct = max(lefts) + 1
    left_all, right_all = refs[:distinct], refs[distinct : distinct + number]
    came_ref = refs[distinct + number] if adds else None
    out_ref = refs[distinct + number + adds]
    scratch = refs[distinct + number + adds + 1 :]
    left_in, right_in, arrived = scratch[:distinct], scratch[distinct : distinct + number], scratch[-1]
    size = out_ref.shape[2]
    columns = pl.ds(pl.multiple_of(bit_ref[0] * size, 128), size)
    left_copies = [pltpu.make_async_copy(left_all[at], left_in[at], arrived.at[at]) for at in range(distinct)]
    right_copies = [
        pltpu.make_async_copy(right_all[at].at[:, columns], right_in[at], arrived.at[distinct + at])
        for at in range(number)
    ]
    started = set()
    for at in range(number):
        if lefts[at] not in started:
            left_copies[lefts[at]].start()
            started.add(lefts[at])
        right_copies[at].start()
    waited = set()
    for at in range(number):
        if lefts[at] not in waited:
            left_copies[lefts[at]].wait()
            waited.add(lefts[at])
        right_copies[at].wait()
        value = dot32(left_in[lefts[at]][...], right_in[at][...], TN)
        blocks = value.shape[0] // 64
        for block in range(blocks):
            if at < number - 1:
                whole_at = at * blocks + block
                holder, row = whole_at // (number - 1), whole_at % (number - 1) * 64
            else:
                holder, row = block, (number - 1) * 64
            index = holder // 4 * 4 + holder % 2 * 2 + holder // 2 % 2
            part = value[block * 64 : (block + 1) * 64]
            if adds:
                part = part + came_ref[index, row : row + 64, :].astype(jnp.float32)
            out_ref[index, row : row + 64, :] = low(part)


def group_outer(bit, lefts, rights, came):
    distinct, indices = [], []
    for left in lefts:
        known = [at for at, other in enumerate(distinct) if other is left]
        if not known:
            known = [len(distinct)]
            distinct.append(left)
        indices.append(known[0])
    number, width = len(rights), lefts[0].shape[1]
    size = width // 2
    adds = came is not None
    outside = pl.BlockSpec(memory_space=pl.ANY)
    shape = (width // 64, 64 * number, size)
    return pl.pallas_call(
        functools.partial(group_outer_kernel, lefts=tuple(indices), number=number, adds=adds),
        grid_spec=pltpu.PrefetchScalarGridSpec(
            num_scalar_prefetch=1,
            grid=(1,),
            in_specs=[outside] * (len(distinct) + number) + [whole(shape)] * adds,
            out_specs=whole(shape),
            scratch_shapes=[pltpu.VMEM(left.shape, jnp.bfloat16) for left in distinct]
            + [pltpu.VMEM((right.shape[0], size), jnp.bfloat16) for right in rights]
            + [pltpu.SemaphoreType.DMA((len(distinct) + number,))],
        ),
        out_shape=jax.ShapeDtypeStruct(shape, jnp.bfloat16),
        compiler_params=pltpu.CompilerParams(vmem_limit_bytes=VMEM_LIMIT),
        cost_estimate=cost(
            sum(2 * right.shape[0] * width * size for right in rights), 2 * sum(right.size for right in rights) * 2
        ),
        name="group_outer",
    )(bit.reshape(1), *distinct, *rights, *([came] if adds else []))


def back_one_kernel(
    dq_ref, gtwo_ref, n_ref, r_ref, wq_ref, wo_ref, gain_ref, gone_ref, gso_ref, gsc_ref, sums_ref
):
    @pl.when(pl.program_id(0) == 0)
    def _():
        sums_ref[...] = jnp.zeros_like(sums_ref)

    queries = dq_ref[...]
    incoming = gtwo_ref[...] + dot32(queries, wq_ref[0], NT)
    normal = n_ref[...]
    add_rows(sums_ref, 0, incoming * normal)
    add_rows(sums_ref, 1, incoming)
    add_rows(sums_ref, 2, queries.astype(jnp.float32))
    grad = norm_back(incoming, normal, r_ref[...], gain_ref[0:1])
    gone_ref[...] = grad
    rounded = low(grad)
    gso_ref[...] = rounded
    add_rows(sums_ref, 3, rounded.astype(jnp.float32))
    gsc_ref[...] = low(dot32(rounded, wo_ref[0], NT))


def back_one(grad_query, grad_two, normal, root, attn_in, attn_out, gain, step):
    count, width = grad_two.shape
    block = rows_of(step, width)
    low_rows = jax.ShapeDtypeStruct((count, width), jnp.bfloat16)
    return pl.pallas_call(
        back_one_kernel,
        grid=(count // step,),
        in_specs=[
            block, block, block, rows_of(step, 1), pick(3, (width, width)), pick(0, (width, width)), whole(gain.shape)
        ],
        out_specs=[block, block, block, whole((8, width))],
        out_shape=[
            jax.ShapeDtypeStruct((count, width), jnp.float32), low_rows, low_rows,
            jax.ShapeDtypeStruct((8, width), jnp.float32),
        ],
        compiler_params=pltpu.CompilerParams(vmem_limit_bytes=VMEM_LIMIT),
        cost_estimate=cost(4 * count * width * width, 18 * count * width + 4 * width * width),
        name="back_one",
    )(grad_query, grad_two, normal, root, attn_in, attn_out, gain)


def pull_kernel(place_ref, *refs, number, adds):
    grads, weights = refs[:number], refs[number : 2 * number]
    own_ref, away_ref = refs[-2:]
    value = refs[2 * number][0] if adds else None
    for grad, weight in zip(grads, weights):
        part = dot32(grad[0], weight[0], NT)
        value = part if value is None else value + part
    mine = pl.program_id(1) == place_ref[0]

    @pl.when(mine)
    def _():
        own_ref[0] = value

    @pl.when(jnp.logical_not(mine))
    def _():
        away_ref[0] = low(value)


def pull_rows(place, grads, weights, indices, base):
    tables, rows, width = grads[0].shape
    half = rows // 2
    number, adds = len(grads), base is not None
    block = pl.BlockSpec((1, half, width), lambda t, h, p: (t, h, 0))
    return pl.pallas_call(
        functools.partial(pull_kernel, number=number, adds=adds),
        grid_spec=pltpu.PrefetchScalarGridSpec(
            num_scalar_prefetch=1,
            grid=(tables, 2),
            in_specs=[block] * number
            + [
                pl.BlockSpec((1, width, width), lambda t, h, p, index=index: (index, 0, 0), pipeline_mode=pl.Buffered(1))
                for index in indices
            ]
            + [block] * adds,
            out_specs=[
                pl.BlockSpec((1, half, width), lambda t, h, p: (p[0] * tables + t, 0, 0)),
                pl.BlockSpec((1, half, width), lambda t, h, p: (t, 0, 0)),
            ],
        ),
        out_shape=[
            jax.ShapeDtypeStruct((2 * tables, half, width), jnp.float32),
            jax.ShapeDtypeStruct((tables, half, width), jnp.bfloat16),
        ],
        compiler_params=pltpu.CompilerParams(vmem_limit_bytes=VMEM_LIMIT),
        cost_estimate=cost(2 * number * tables * rows * width * width, 2 * number * (tables * rows * width + width * width) + 6 * tables * rows * width),
        name="pull_rows",
    )(place.reshape(1), *grads, *([weights] * number), *([base] if adds else []))


def after(value, *others):
    return lax.optimization_barrier((value, *others))[0]


def on_device_tables(
    target_in,
    memory,
    cotangent,
    target_len,
    memory_len,
    attn_in,
    attn_out,
    biases,
    norm_gain,
    norm_bias,
    up_weight,
    up_bias,
    down_weight,
):
    place = lax.axis_index("seq")
    item = lax.axis_index("items")
    core, y_at, z_low, z_high = item & 1, (item >> 1) & 1, (item >> 2) & 1, (item >> 3) & 1
    tables = target_in.shape[0] // 2
    width = target_in.shape[2]
    half_hidden = up_weight.shape[1]
    swap_core, swap_y, swap_low, swap_high = (
        functools.partial(swap_items, bit=bit) for bit in (1, 2, 4, 8)
    )
    own_tables = lambda value: lax.dynamic_slice_in_dim(value, place * tables, tables, 0)
    other_tables = lambda value: lax.dynamic_slice_in_dim(value, (1 - place) * tables, tables, 0)

    def place_rows(own, came):
        return lax.dynamic_update_slice_in_dim(own, came.astype(own.dtype), (1 - place) * tables, 0)

    def split(value, axis, bit):
        return (
            lax.dynamic_index_in_dim(value, bit, axis, keepdims=False),
            lax.dynamic_index_in_dim(value, 1 - bit, axis, keepdims=False),
        )

    slices = width // lax.axis_size("items")
    own_slice = lambda value: lax.dynamic_slice_in_dim(value, item * slices, slices, 0)
    sent = swap_seq(jnp.concatenate([own_slice(up_weight), own_slice(down_weight)], 0))
    up_other = lax.all_gather(sent[:slices], "items", axis=0, tiled=True)
    down_other = lax.all_gather(sent[slices:], "items", axis=0, tiled=True)
    target_came = swap_seq(other_tables(target_in))
    memory_came = swap_seq(other_tables(memory))
    up_bias_other = swap_seq(up_bias)
    cotangent_came = swap_seq(after(other_tables(cotangent), target_came))
    target_lengths, memory_lengths = own_tables(target_len[0]), own_tables(memory_len[0])

    by_table = lambda value: value.reshape(tables, -1, width)
    flat = lambda value: value.reshape(-1, width)
    none, ones = jnp.zeros_like(biases[0]), jnp.ones_like(biases[0])
    scale = jnp.stack([ones * (0.125 * LOG2E), ones, ones])
    self_stack, target_rows = project_halves(
        place, own_tables(target_in), target_came, attn_in, 0, jnp.stack([biases[0], none, biases[1]]), scale
    )
    rows = self_stack.shape[2]
    half = rows // 2
    self_at, cross_at = (0, 1, 2), (0, 0, 1)
    self_context, self_total = attend(
        target_lengths, self_stack, self_stack, self_stack, self_at, rows, True
    )
    normal_one, root_one, norm_one_low, cross_query = mix(
        flat(self_context), target_rows, attn_out, attn_in, biases, norm_gain, norm_bias, 256
    )
    cross_stack, memory_rows = project_halves(
        place, own_tables(memory), memory_came, attn_in, 4, jnp.stack([none, biases[4]]), scale[1:]
    )
    cross_query = by_table(cross_query)[None]
    cross_context, cross_total = attend(
        memory_lengths, cross_query, cross_stack, cross_stack, cross_at, half, False
    )
    (
        layer_own, layer_away, ffn_right, ffn_left, grad_two, grad_cross_out, grad_cross_context, ffn_sums, up_bias_sums
    ) = ffn(
        place, flat(cross_context), normal_one, own_tables(cotangent), cotangent_came, attn_out,
        up_weight, up_other, down_weight, down_other, up_bias, up_bias_other, biases, norm_gain, norm_bias, 1024,
    )
    layer_out = place_rows(layer_own, swap_seq(layer_away))

    up_away = ffn_outer(1 - core, ffn_left, ffn_right, 0, None, 512)
    up_came = swap_core(up_away)
    down_away = ffn_outer(1 - core, after(ffn_left, up_away), ffn_right, 1, None, 512)
    down_came = swap_core(down_away)
    blocks = lambda value: value.reshape(2, 2, 2, 2 * slices, half_hidden)
    up_part = blocks(ffn_outer(core, after(ffn_left, down_away), ffn_right, 0, up_came, 512))
    up_keep, up_send = split(up_part, 2, y_at)
    up_came = swap_y(up_send)
    down_part = blocks(ffn_outer(core, after(ffn_left, up_send), ffn_right, 1, down_came, 512))
    down_keep, down_send = split(down_part, 1, z_low)
    down_came = swap_low(down_send)

    grad_cross_query, grad_cross_keys, grad_cross_values = attend_back(
        memory_lengths, cross_query, cross_stack, cross_stack, cross_at,
        after(by_table(grad_cross_context), down_send), cross_context, cross_total, half, False,
    )
    up_keep, up_send = split(add_low(up_keep, after(up_came, grad_cross_query)), 1, z_low)
    up_came = swap_low(up_send)
    down_keep, down_send = split(add_low(down_keep, after(down_came, grad_cross_query)), 1, y_at)
    down_came = swap_y(down_send)

    cross_lefts = (norm_one_low, memory_rows, memory_rows, flat(cross_context))
    cross_rights = (
        after(flat(grad_cross_query), up_send, down_send), flat(grad_cross_keys), flat(grad_cross_values), grad_cross_out
    )
    group_away = group_outer(1 - core, cross_lefts, cross_rights, None)
    group_came = swap_core(group_away)
    memory_own, memory_away = pull_rows(
        place, [grad_cross_keys, after(grad_cross_values, group_away)], attn_in, (4, 5), None
    )
    memory_came = swap_seq(memory_away)

    ffn_part = jnp.stack([add_low(up_keep, after(up_came, memory_away)), add_low(down_keep, after(down_came, memory_away))])
    ffn_keep, ffn_send = ffn_part[..., : half_hidden // 2], ffn_part[..., half_hidden // 2 :]
    ffn_came = swap_seq(ffn_send)
    holders = lambda value: value.reshape(2, 2, 2, 2, -1, width // 2)
    cross_part = holders(group_outer(core, cross_lefts, (after(cross_rights[0], ffn_send),) + cross_rights[1:], group_came))

    def first_stage(part):
        size = part.shape[4] // 2
        one_keep, one_send = split(part[:, :, :, :, :size], 1, y_at)
        two_keep, two_send = split(part[:, :, :, :, size:], 0, z_low)
        return one_keep, two_keep, one_send, two_send

    def second_stage(kept, came):
        one_keep, one_send = split(add_low(kept[0], came[0]), 0, z_low)
        two_keep, two_send = split(add_low(kept[1], came[1]), 0, y_at)
        return one_keep, two_keep, one_send, two_send

    def third_stage(kept, came):
        return split(jnp.concatenate([add_low(kept[0], came[0]), add_low(kept[1], came[1])], 2), 0, place)

    *cross_kept, one_send, two_send = first_stage(cross_part)
    cross_came = swap_y(one_send), swap_low(two_send)
    grad_one, grad_self_out, grad_self_context, one_sums = back_one(
        after(flat(grad_cross_query), one_send, two_send), grad_two, normal_one, root_one, attn_in, attn_out, norm_gain, 256
    )
    grad_self_query, grad_self_keys, grad_self_values = attend_back(
        target_lengths, self_stack, self_stack, self_stack, self_at,
        by_table(grad_self_context), self_context, self_total, half, True,
    )
    self_lefts = (target_rows, target_rows, target_rows, flat(self_context))
    self_rights = (flat(grad_self_query), flat(grad_self_keys), flat(grad_self_values), grad_self_out)
    group_away = group_outer(1 - core, self_lefts, self_rights, None)
    group_came = swap_core(group_away)
    *cross_kept, one_send, two_send = second_stage(cross_kept, [after(value, group_away) for value in cross_came])
    cross_came = swap_low(one_send), swap_y(two_send)
    ffn_keep, ffn_send = split(add_low(ffn_keep, after(ffn_came, group_away)), 1, z_high)
    ffn_came = swap_high(ffn_send)
    target_own, target_away = pull_rows(
        place,
        [after(grad_self_query, one_send, two_send, ffn_send), grad_self_keys, grad_self_values],
        attn_in, (0, 1, 2), by_table(grad_one),
    )
    target_came = swap_seq(target_away)
    self_part = holders(
        group_outer(core, self_lefts, (after(self_rights[0], target_away),) + self_rights[1:], group_came)
    )
    *self_kept, one_send, two_send = first_stage(self_part)
    self_came = swap_y(one_send), swap_low(two_send)
    cross_keep, cross_send = third_stage(cross_kept, [after(value, one_send, two_send) for value in cross_came])
    cross_part = add_low(cross_keep, swap_seq(cross_send))
    *self_kept, one_send, two_send = second_stage(self_kept, self_came)
    self_keep, self_send = third_stage(self_kept, (swap_low(one_send), swap_y(two_send)))
    self_part = add_low(self_keep, swap_seq(self_send))
    own = jnp.where(z_high == 1, cross_part, self_part)
    away = jnp.where(z_high == 1, self_part, cross_part)
    keep, send = split(add_low(own, swap_high(away)), 0, core)
    side_by_side = lambda own, came: jnp.where(
        core == 0, jnp.concatenate([own, came], -1), jnp.concatenate([came, own], -1)
    )
    shard = side_by_side(keep, swap_core(send)).astype(jnp.float32)
    inner_rows = 6 * width // (2 * lax.axis_size("items"))
    attn_in_grad, attn_out_grad = shard[:inner_rows], shard[inner_rows:]
    ffn_keep, ffn_send = split(add_low(ffn_keep, ffn_came).reshape(2, 2, slices, half_hidden // 2), 1, core)
    ffn_shard = side_by_side(ffn_keep, swap_core(ffn_send)).astype(jnp.float32)
    target_grad = place_rows(target_own, target_came)
    memory_grad = place_rows(memory_own, memory_came)

    up_mine, up_rest = up_bias_sums[0, :half_hidden], up_bias_sums[0, half_hidden:]
    up_bias_total = jnp.where(
        place == 0, jnp.concatenate([up_mine, up_rest]), jnp.concatenate([up_rest, up_mine])
    )
    small = jnp.concatenate(
        [
            jnp.stack(
                [
                    total32(flat(grad_self_query)), total32(flat(grad_self_values)), one_sums[3],
                    one_sums[2], total32(flat(grad_cross_values)), ffn_sums[5], ffn_sums[2],
                    one_sums[0], ffn_sums[3], ffn_sums[0], one_sums[1], ffn_sums[4], ffn_sums[1],
                ]
            ),
            up_bias_total.reshape(-1, width),
        ],
        0,
    )
    for swap in (swap_core, swap_y, swap_low, swap_high, swap_seq):
        small = small + swap(small)
    return (
        layer_out,
        target_grad,
        memory_grad,
        attn_in_grad,
        attn_out_grad,
        small[:7],
        small[7:10],
        small[10:13],
        ffn_shard[0],
        small[13:].reshape(-1),
        ffn_shard[1],
    )


def solution(mesh):
    in_specs = (
        P("items", "seq", None),
        P("items", "seq", None),
        P("items", "seq", None),
        P("items", None),
        P("items", None),
        P(),
        P(),
        P(),
        P(),
        P(),
        P(None, "seq"),
        P("seq"),
        P(None, "seq"),
    )
    out_specs = (
        P("items", "seq", None),
        P("items", "seq", None),
        P("items", "seq", None),
        P(("items", "seq"), None),
        P(("items", "seq"), None),
        P(),
        P(),
        P(),
        P("items", "seq"),
        P(),
        P("items", "seq"),
    )
    whole_tables = mesh.shape["seq"] == 2 and mesh.shape["items"] == 16
    plan = on_device_tables if whole_tables else on_device
    return jax.shard_map(
        plan, mesh=mesh, in_specs=in_specs, out_specs=out_specs, check_vma=False
    )
```
